768 devices in a mesh: row: 24 (over x, z_lo), col: 32 (over z_hi, y, core).
Axes of the slice: x: 4, y: 8, z: 12 (z_hi: 2, z_lo: 6; z = z_hi * 6 + z_lo), core: 2. Of those that a mesh axis runs over, the one named last changes fastest.
Arguments:
- left_factor: bfloat16 [32768, 12288], P('col', 'row'), may hold values from -6 to 6
- left_mask: int32 [256, 96], P('col', 'row'), may hold values from 0 to 1, as said below
- right_factor: bfloat16 [16384, 24576], P('col', 'row'), may hold values from -0.5 to 0.5
- right_mask: int32 [128, 192], P('col', 'row'), may hold values from 0 to 1, as said below
Outputs:
- window_product: bfloat16 [32768, 24576], P('col', 'row')
The draws below stay inside these ranges and needn't reach their ends.
Inputs may be any that keep to these rules, and one draw needn't show every extreme that they name: `left_mask`: 1 marks an occupied tile; one device's piece of 8 x 4 tiles holds at most 12 ones, and some piece holds exactly 12. `right_mask`: 1 marks an occupied tile; one device's piece of 4 x 8 tiles holds at most 12 ones, and some piece holds exactly 12.
All inputs are finite; a program needn't handle non-finite values.
Results may differ from the reference program's by a relative error of at most 0.001.
Values may be sent and summed in bfloat16 or wider, within the bound.
No kernel may reach another device: no remote copies, remote signals or barrier semaphores. Data moves between devices by JAX's collectives and lax.ppermute only.
A program may use at most 64 MiB of HBM per device.

```python
import jax
import jax.numpy as jnp
from jax import lax

TILE = 128
TB = 8
KT = 4
STEPS = 4
OCC = 12
ROWS = 32768
COLS = 24576
INNER_LEFT = 12288
INNER_RIGHT = 16384
N_ROW = 24
N_COL = 32


def occupancy(key, blocks_down, blocks_across, tile_rows, tile_cols):
    light_key, busy_key, which_key, pick_key, order_key = jax.random.split(key, 5)
    pieces = blocks_down * blocks_across
    light = jax.random.randint(light_key, (pieces,), max(1, OCC // 4), max(1, OCC // 2) + 1)
    busy = jax.random.randint(busy_key, (pieces,), max(1, 3 * OCC // 4), OCC + 1)
    heavy = jax.random.randint(which_key, (pieces,), 0, 8) == 0
    counts = jnp.where(heavy, busy, light)
    chosen = jax.random.randint(pick_key, (), 0, pieces)
    counts = jnp.where(jnp.arange(pieces) == chosen, OCC, counts)
    order_keys = jax.random.split(order_key, pieces)
    ranking = jax.vmap(lambda one_key: jax.random.permutation(one_key, tile_rows * tile_cols))(order_keys)
    occupied = (ranking < counts[:, None]).astype(jnp.int32)
    occupied = occupied.reshape(blocks_down, blocks_across, tile_rows, tile_cols).transpose(0, 2, 1, 3)
    return occupied.reshape(blocks_down * tile_rows, blocks_across * tile_cols)


def draw_left_mask(key, part):
    key = jax.random.fold_in(key, 11)
    return occupancy(key, N_COL, N_ROW, TB, KT)


def draw_right_mask(key, part):
    key = jax.random.fold_in(key, 23)
    return occupancy(key, N_COL, N_ROW, KT, TB)


def block_scale(stream_key, shape, cuts, smallest, high):
    factor_of = 1.0
    for dim, parts in cuts:
        draws = jax.random.uniform(jax.random.fold_in(jax.random.fold_in(stream_key, 6), dim), (parts,), jnp.float32, smallest / len(cuts), high / len(cuts))
        factor_of = factor_of * jnp.repeat(jnp.exp(draws), shape[dim] // parts).reshape((-1,) + (1,) * (len(shape) - 1 - dim))
    return factor_of


def bell_draw(rng, extent, scale, bound, cuts=(), kind=jnp.bfloat16):
    array = scale * jax.random.normal(rng, extent, jnp.float32)
    if cuts:
        array = array * block_scale(rng, extent, cuts, -0.22, 0.18)
    return jnp.clip(array, -bound, bound).astype(kind)


def setup_inputs(seed: int = 0) -> dict:
    seeds = jax.random.split(jax.random.key(seed), 5)
    return {
        "left_factor": bell_draw(seeds[0], (ROWS, INNER_LEFT), 1.0, 6.0, ((0, 32), (1, 24))),
        "left_mask": draw_left_mask(jax.random.fold_in(seeds[4], 71), 0),
        "right_factor": bell_draw(seeds[2], (INNER_RIGHT, COLS), TILE ** -0.5, 0.5, ((0, 32), (1, 24))),
        "right_mask": draw_right_mask(jax.random.fold_in(seeds[4], 71), 0),
    }


def apply_mask(tile_mask, block_data):
    expanded = jnp.repeat(jnp.repeat(tile_mask, TILE, axis=0), TILE, axis=1)
    return block_data * expanded.astype(block_data.dtype)


def reference(left_factor, left_mask, right_factor, right_mask):
    left_masked = apply_mask(left_mask, left_factor).reshape(N_COL, TB * TILE, N_ROW, KT * TILE)
    right_masked = apply_mask(right_mask, right_factor).reshape(N_COL, KT * TILE, N_ROW, TB * TILE)

    def block_row(block_index):
        total = jnp.zeros((TB * TILE, N_ROW, TB * TILE), jnp.float32)
        left_row = lax.dynamic_index_in_dim(left_masked, block_index, 0, keepdims=False).astype(jnp.float32)
        for step in range(STEPS):
            left_part = jnp.roll(left_row, -step, axis=1)
            source = ((block_index + step) % N_COL).astype(jnp.int32)
            right_part = lax.dynamic_index_in_dim(right_masked, source, 0, keepdims=False).astype(jnp.float32)
            total = total + jnp.einsum("iqk,kqj->iqj", left_part, right_part)
        return total.reshape(TB * TILE, N_ROW * TB * TILE).astype(jnp.bfloat16)

    stacked = lax.map(block_row, jnp.arange(N_COL, dtype=jnp.int32))
    return stacked.reshape(N_COL * TB * TILE, N_ROW * TB * TILE)
```

```python
import jax
import jax.numpy as jnp
from jax import lax
from jax.experimental import pallas as pl
from jax.experimental.pallas import tpu as pltpu
from jax.sharding import PartitionSpec as P

TILE = 128
TB = 8
KT = 4
OCC = 12
HEAD = 16
PACK = OCC * TILE + HEAD
EMPTY = 64.0
VMEM_LIMIT = 32 * 1024 * 1024


def number_slots(mask_at, tile_rows, tile_cols, slots):
    for j in range(OCC):
        slots[j] = 0
    count = jnp.int32(0)
    for i in range(tile_rows):
        for k in range(tile_cols):
            occupied = mask_at(i, k) != 0

            @pl.when(occupied & (count < OCC))
            def _():
                slots[count] = i * tile_cols + k

            count = count + occupied.astype(jnp.int32)
    return jnp.minimum(count, OCC)


def pack_one(mask_at, source, packed, slots, sem, tile_rows, tile_cols):
    count = number_slots(mask_at, tile_rows, tile_cols, slots)
    copies = []
    for j in range(OCC):
        tile = slots[j]
        i = pl.multiple_of(tile // tile_cols * TILE, TILE)
        k = pl.multiple_of(tile % tile_cols * TILE, TILE)
        copy = pltpu.make_async_copy(
            source.at[pl.ds(i, TILE), pl.ds(k, TILE)],
            packed.at[pl.ds(j * TILE, TILE), :],
            sem.at[j],
        )
        copy.start()
        copies.append(copy)
    lane = lax.broadcasted_iota(jnp.int32, (HEAD, TILE), 1)
    head = jnp.full((HEAD, TILE), EMPTY, jnp.float32)
    for j in range(OCC):
        here = (lane == j) & (j < count)
        head = jnp.where(here, slots[j].astype(jnp.float32), head)
    packed[OCC * TILE : PACK, :] = head.astype(jnp.bfloat16)
    return copies


def pack_kernel(left_mask_across, right_mask, left, right, left_packed, right_packed, slots, sem):
    copies = pack_one(lambda i, k: right_mask[i, k], right, right_packed, slots, sem.at[0], KT, TB)
    copies += pack_one(lambda i, k: left_mask_across[k, i], left, left_packed, slots, sem.at[1], TB, KT)
    for copy in copies:
        copy.wait()


def pack(left_mask, right_mask, left, right):
    smem = pl.BlockSpec(memory_space=pltpu.SMEM)
    hbm = pl.BlockSpec(memory_space=pltpu.HBM)
    vmem = pl.BlockSpec(memory_space=pltpu.VMEM)
    shape = jax.ShapeDtypeStruct((PACK, TILE), jnp.bfloat16)
    return pl.pallas_call(
        pack_kernel,
        out_shape=(shape, shape),
        in_specs=[smem, smem, hbm, hbm],
        out_specs=(vmem, vmem),
        scratch_shapes=[pltpu.SMEM((OCC,), jnp.int32), pltpu.SemaphoreType.DMA((2, OCC))],
        compiler_params=pltpu.CompilerParams(vmem_limit_bytes=VMEM_LIMIT),
        cost_estimate=pl.CostEstimate(flops=0, bytes_accessed=2 * 1024 * 1024, transcendentals=0),
        name="pack",
    )(left_mask.T, right_mask, left, right)


def unpack(packed, dense, tile_cols):
    dense[...] = jnp.zeros_like(dense)
    head = packed[OCC * TILE : PACK, :].astype(jnp.float32).astype(jnp.int32)
    for j in range(OCC):
        tile = head[0, j]

        @pl.when(tile < TB * KT)
        def _():
            i = pl.multiple_of(tile // tile_cols * TILE, TILE)
            k = pl.multiple_of(tile % tile_cols * TILE, TILE)
            dense[pl.ds(i, TILE), pl.ds(k, TILE)] = packed[j * TILE : (j + 1) * TILE, :]


ROWS_AT_ONCE = 256


def step_kernel(*refs, first, last):
    if first:
        left_packed, right_packed, out, left, right = refs
    else:
        total, left_packed, right_packed, out, left, right = refs
    unpack(left_packed, left, KT)
    unpack(right_packed, right, TB)

    @pl.loop(0, TB * TILE // ROWS_AT_ONCE)
    def _(block):
        rows = pl.ds(pl.multiple_of(block * ROWS_AT_ONCE, ROWS_AT_ONCE), ROWS_AT_ONCE)
        part = jnp.dot(left[rows, :], right[...], preferred_element_type=jnp.float32)
        if not first:
            part = total[rows, :] + part
        out[rows, :] = part.astype(out.dtype)


def multiply(total, left_packed, right_packed, last):
    first = total is None
    vmem = pl.BlockSpec(memory_space=pltpu.VMEM)
    args = ([] if first else [total]) + [left_packed, right_packed]
    kind = jnp.bfloat16 if last else jnp.float32
    side = TB * TILE

    def kernel(*refs):
        step_kernel(*refs, first=first, last=last)

    return pl.pallas_call(
        kernel,
        out_shape=jax.ShapeDtypeStruct((side, side), kind),
        in_specs=[vmem] * len(args),
        out_specs=vmem,
        scratch_shapes=[
            pltpu.VMEM((side, KT * TILE), jnp.bfloat16),
            pltpu.VMEM((KT * TILE, side), jnp.bfloat16),
        ],
        compiler_params=pltpu.CompilerParams(vmem_limit_bytes=VMEM_LIMIT),
        cost_estimate=pl.CostEstimate(
            flops=2 * side * side * KT * TILE, bytes_accessed=2 * 1024 * 1024, transcendentals=0
        ),
        name="multiply",
    )(*args)


def shifted(block, axis, distance):
    size = lax.axis_size(axis)
    return lax.ppermute(block, axis, [((i + distance) % size, i) for i in range(size)])


def local(left_factor, left_mask, right_factor, right_mask):
    left, right = pack(left_mask, right_mask, left_factor, right_factor)
    lefts, rights = [left], [right]
    for _ in range(3):
        rights.append(shifted(rights[-1], "col", 1))
        lefts.append(shifted(lefts[-1], "row", 1))
    total = None
    for step in range(4):
        total = multiply(total, lefts[step], rights[step], step == 3)
    return total


def solution(mesh):
    placed = (P("col", "row"), P("col", "row"), P("col", "row"), P("col", "row"))
    return jax.shard_map(
        local, mesh=mesh, in_specs=placed, out_specs=P("col", "row"), check_vma=False
    )
```

```python
import jax
import jax.numpy as jnp
from jax import lax
from jax.experimental import pallas as pl
from jax.experimental.pallas import tpu as pltpu
from jax.sharding import PartitionSpec as P

TILE = 128
TB = 8
KT = 4
OCC = 12
HEAD = 16
PACK = OCC * TILE + HEAD
CUT = OCC // 2 * TILE
EMPTY = 64.0
SIDE = TB * TILE
DEPTH = KT * TILE
BLOCK = 256
VMEM_LIMIT = 20 * 1024 * 1024
PACK_VMEM = 60 * 1024 * 1024
VMEM = pl.BlockSpec(memory_space=pltpu.VMEM)
SMEM = pl.BlockSpec(memory_space=pltpu.SMEM)
HBM = pl.BlockSpec(memory_space=pltpu.HBM)
COST = pl.CostEstimate(flops=1, bytes_accessed=1, transcendentals=0)

X, Y, Z = 4, 8, 12
RUN = 6
HALF_LOOP = 16
N_COL = 32


def device(x, y, z, core):
    z = z % Z
    return (x * RUN + z % RUN) * N_COL + (z // RUN) * HALF_LOOP + (y % Y) * 2 + core


def per_line(*routes):
    return [
        (device(x, y, z, core), device(x, to_y, z + dz, to_core))
        for x in range(X)
        for z in range(Z)
        for (y, core), (to_y, to_core), dz in routes
    ]


def over(source, target):
    (from_dx, from_z), (to_dx, to_z) = source, target
    return [
        (((x + from_dx) % X * RUN + from_z) * N_COL + c, ((x + to_dx) % X * RUN + to_z) * N_COL + c)
        for x in range(X)
        for c in range(N_COL)
    ]


def down(top):
    return [pair for z in range(top) for pair in over((0, z + 1), (0, z))]


def right_hop(distance, within):
    return [
        (q * N_COL + half * HALF_LOOP + c + distance, q * N_COL + half * HALF_LOOP + c)
        for q in range(X * RUN)
        for half in range(2)
        for c in range(within - distance)
    ]


def send(block, route):
    return lax.ppermute(block, ("row", "col"), route)


def after(block, *others):
    return lax.optimization_barrier((block, *others))[0]


def number_slots(mask_at, tile_rows, tile_cols, slots):
    for j in range(OCC):
        slots[j] = 0
    count = jnp.int32(0)
    for i in range(tile_rows):
        for k in range(tile_cols):
            occupied = mask_at(i, k) != 0

            @pl.when(occupied & (count < OCC))
            def _():
                slots[count] = i * tile_cols + k

            count = count + occupied.astype(jnp.int32)
    return jnp.minimum(count, OCC)


def tile_at(tile, tile_cols):
    i = pl.multiple_of(tile // tile_cols * TILE, TILE)
    k = pl.multiple_of(tile % tile_cols * TILE, TILE)
    return pl.ds(i, TILE), pl.ds(k, TILE)


def gather_tiles(source, slots, count, tile_cols, outs):
    lane = lax.broadcasted_iota(jnp.int32, (HEAD, TILE), 1)
    head = jnp.full((HEAD, TILE), EMPTY, jnp.float32)
    for j in range(OCC):
        tile = slots[j]
        data = source[tile_at(tile, tile_cols)]
        for out, base in outs:
            at = j * TILE - base
            if 0 <= at <= out.shape[0] - TILE:
                out[at : at + TILE, :] = data
        head = jnp.where((lane == j) & (j < count), tile.astype(jnp.float32), head)
    for out, base in outs:
        if base + out.shape[0] == PACK:
            out[out.shape[0] - HEAD :, :] = head.astype(jnp.bfloat16)


def pack_kernel(left_mask_across, right_mask, left, right, *refs):
    left_a, left_b, left_all, right_all, left_here, right_here, slots, sems = refs
    left_copy = pltpu.make_async_copy(left, left_here, sems.at[0])
    right_copy = pltpu.make_async_copy(right, right_here, sems.at[1])
    left_copy.start()
    right_copy.start()
    left_count = number_slots(lambda i, k: left_mask_across[k, i], TB, KT, slots.at[0])
    right_count = number_slots(lambda i, k: right_mask[i, k], KT, TB, slots.at[1])
    left_copy.wait()
    gather_tiles(left_here, slots.at[0], left_count, KT, [(left_a, 0), (left_b, CUT), (left_all, 0)])
    right_copy.wait()
    gather_tiles(right_here, slots.at[1], right_count, TB, [(right_all, 0)])


def pack(left_mask, right_mask, left, right):
    return pl.pallas_call(
        pack_kernel,
        out_shape=tuple(jax.ShapeDtypeStruct((n, TILE), jnp.bfloat16) for n in (CUT, PACK - CUT, PACK, PACK)),
        in_specs=[SMEM, SMEM, HBM, HBM],
        out_specs=(VMEM,) * 4,
        scratch_shapes=[
            pltpu.VMEM((SIDE, DEPTH), jnp.bfloat16),
            pltpu.VMEM((DEPTH, SIDE), jnp.bfloat16),
            pltpu.SMEM((2, OCC), jnp.int32),
            pltpu.SemaphoreType.DMA((2,)),
        ],
        compiler_params=pltpu.CompilerParams(vmem_limit_bytes=PACK_VMEM),
        cost_estimate=COST,
        name="pack",
    )(left_mask.T, right_mask, left, right)


def one_of(value, members):
    found = value < 0
    for member in members:
        found = found | (value == member)
    return found


def places_of(choice, wanted):
    z = lax.axis_index("row") % RUN
    c = lax.axis_index("col") % HALF_LOOP
    here = z < 0
    at_c = {at: tuple(k for k in range(HALF_LOOP) if choice[at, k] in wanted) for at in range(RUN)}
    for members in sorted(set(at_c.values())):
        if members:
            rows = one_of(z, [at for at in range(RUN) if at_c[at] == members])
            here = here | (rows if len(members) == HALF_LOOP else rows & one_of(c, members))
    return here


def pick(choice, pieces, use):
    for n, piece in enumerate(pieces):

        @pl.when(places_of(choice, {n}))
        def _(piece=piece):
            use(piece)


def whole(array):
    return ((array, 0), (array, CUT))


def halves(first, second):
    return ((first, 0), (second, 0))


def choose(of):
    arrays, pieces, choice = [], [], {}

    def number(array):
        known = [n for n, other in enumerate(arrays) if other is array]
        if not known:
            arrays.append(array)
        return known[0] if known else len(arrays) - 1

    for z in range(RUN):
        for c in range(HALF_LOOP):
            piece = of(z, c)
            if piece is None:
                choice[z, c] = None
                continue
            piece = tuple((number(array), base) for array, base in piece)
            if piece not in pieces:
                pieces.append(piece)
            choice[z, c] = pieces.index(piece)
    return arrays, pieces, choice


def rows_of(piece, first, n):
    ref, base = piece[first >= CUT]
    first = first - CUT * (first >= CUT) + base
    return ref[first : first + n, :]


def spread_all(work, heads, numbers, sem):
    for n, (choice, refs, _, _) in enumerate(work):

        def read(packed, n=n):
            heads[n] = rows_of(packed, OCC * TILE, HEAD).astype(jnp.float32).astype(jnp.int32)[:8]

        pick(choice, refs, read)
    copy = pltpu.make_async_copy(heads, numbers, sem)
    copy.start()
    for choice, _, dense, _ in work:

        @pl.when(jnp.logical_not(places_of(choice, {None})))
        def _(dense=dense):
            dense[...] = jnp.zeros_like(dense)

    copy.wait()
    for n, (choice, refs, dense, tile_cols) in enumerate(work):

        def place(packed, n=n, dense=dense, tile_cols=tile_cols):
            for j in range(OCC):
                tile = numbers[n, 0, j]

                @pl.when(tile < TB * KT)
                def _():
                    dense[tile_at(tile, tile_cols)] = rows_of(packed, j * TILE, TILE)

        pick(choice, refs, place)


def head_scratch(n):
    return [
        pltpu.VMEM((n, 8, TILE), jnp.int32),
        pltpu.SMEM((n, 8, TILE), jnp.int32),
        pltpu.SemaphoreType.DMA(()),
    ]


def take(refs, n):
    return [refs.pop(0) for _ in range(n)]


def take_pieces(refs, chosen):
    arrays, pieces, _ = chosen
    here = take(refs, len(arrays))
    return [tuple((here[n], base) for n, base in piece) for piece in pieces]


def multiply(total, steps, last):
    first, n = total is None, len(steps)
    skips = [step[0][2] for step in steps]
    sometimes = [at for at in range(n) if None in skips[at].values()]
    always = n - len(sometimes)
    assert sometimes == list(range(always, n))

    def kernel(*refs):
        refs = list(refs)
        before = None if first else refs.pop(0)
        inputs = [(take_pieces(refs, left), take_pieces(refs, right)) for left, right in steps]
        out, left, right, heads, numbers, sem = take(refs, 6)
        work = []
        for at, (left_in, right_in) in enumerate(inputs):
            inner = pl.ds(at * DEPTH, DEPTH)
            work.append((steps[at][0][2], left_in, left.at[:, inner], KT))
            work.append((steps[at][1][2], right_in, right.at[inner, :], TB))
        spread_all(work, heads, numbers, sem)
        rounded, sems = refs if last else (None, None)

        def add_up(rows, depth, then):
            part = jnp.dot(left[rows, :depth], right[:depth, :], preferred_element_type=jnp.float32)
            then(rows, part if first else before[rows, :] + part)

        def each_block(depth, then):
            for block in range(SIDE // BLOCK):
                add_up(pl.ds(block * BLOCK, BLOCK), depth, then)

        def keep(rows, value):
            out[rows, :] = value

        def write(rows, value):
            at = rows.start // BLOCK
            rounded[rows, :] = value.astype(jnp.bfloat16)
            pltpu.make_async_copy(rounded.at[rows, :], out.at[rows, :], sems.at[at]).start()

        then = write if last else keep
        if sometimes:
            skipped = places_of(skips[always], {None})

            @pl.when(skipped)
            def _():
                each_block(always * DEPTH, then)

            @pl.when(jnp.logical_not(skipped))
            def _():
                each_block(n * DEPTH, then)

        else:
            each_block(n * DEPTH, then)
        if last:
            for block in range(SIDE // BLOCK):
                rows = pl.ds(block * BLOCK, BLOCK)
                pltpu.make_async_copy(rounded.at[rows, :], out.at[rows, :], sems.at[block]).wait()

    args = [] if first else [total]
    for left, right in steps:
        args += left[0] + right[0]
    scratch = [
        pltpu.VMEM((SIDE, n * DEPTH), jnp.bfloat16),
        pltpu.VMEM((n * DEPTH, SIDE), jnp.bfloat16),
    ] + head_scratch(2 * n)
    if last:
        scratch += [
            pltpu.VMEM((SIDE, SIDE), jnp.bfloat16),
            pltpu.SemaphoreType.DMA((SIDE // BLOCK,)),
        ]
    return pl.pallas_call(
        kernel,
        out_shape=jax.ShapeDtypeStruct((SIDE, SIDE), jnp.bfloat16 if last else jnp.float32),
        in_specs=[VMEM] * len(args),
        out_specs=HBM if last else VMEM,
        scratch_shapes=scratch,
        compiler_params=pltpu.CompilerParams(vmem_limit_bytes=VMEM_LIMIT),
        cost_estimate=COST,
        name="finish" if last else "multiply",
    )(*args)


def local(left_factor, left_mask, right_factor, right_mask):
    la, lb, l0, r0 = pack(left_mask, right_mask, left_factor, right_factor)

    ring = down(5) + over((1, 0), (0, 5))
    first_a, first_b = send(la, ring), send(lb, ring)
    over_both = send(l0, over((1, 1), (0, 5)) + over((1, 2), (0, 4)))
    second_a, second_b = send(first_a, down(5)), send(first_b, down(5))
    moved = send(r0, per_line(((0, 1), (7, 1), 0), ((0, 0), (0, 1), 0), ((1, 0), (1, 1), 0)))
    crossed = send(moved, per_line(((0, 1), (7, 0), 6), ((7, 1), (7, 1), 6), ((1, 1), (6, 0), 6)))
    n1 = send(r0, right_hop(1, 16))
    n2 = send(r0, right_hop(2, 16))
    n3 = send(n2, right_hop(1, 14))

    def early(c):
        return c < 15

    lefts = {
        1: [halves(first_a, first_b)] * 6,
        2: [halves(second_a, second_b)] * 5 + [whole(over_both)],
    }
    total = multiply(
        None,
        [
            (choose(lambda z, c: whole(l0)), choose(lambda z, c: whole(r0))),
            (
                choose(lambda z, c: lefts[1][z] if early(c) else None),
                choose(lambda z, c: whole(n1) if early(c) else None),
            ),
        ],
        False,
    )
    third = send(after(jnp.concatenate([second_a, second_b]), over_both), down(4))
    changed = send(over_both, over((0, 5), (0, 4)) + over((0, 4), (0, 5)))
    lefts[3] = [whole(third)] * 4 + [whole(changed)] * 2
    crossed_late = after(crossed, over_both)
    g1 = send(crossed_late, per_line(((7, 0), (7, 1), 0)))
    g2 = send(crossed_late, per_line(((7, 0), (6, 1), 0), ((7, 1), (7, 0), 0), ((6, 0), (7, 1), 0)))

    def right_of(step, c):
        return whole({1: (n1, g1), 2: (n2, crossed), 3: (n3, g2)}[step][c + step >= HALF_LOOP])

    steps = [
        (choose(lambda z, c: lefts[step][z]), choose(lambda z, c: right_of(step, c))) for step in (2, 3)
    ]
    steps.append(
        (
            choose(lambda z, c: None if early(c) else lefts[1][z]),
            choose(lambda z, c: None if early(c) else right_of(1, c)),
        )
    )
    return multiply(total, steps, True)


def solution(mesh):
    placed = (P("col", "row"), P("col", "row"), P("col", "row"), P("col", "row"))
    return jax.shard_map(
        local, mesh=mesh, in_specs=placed, out_specs=P("col", "row"), check_vma=False
    )
```

```python
import jax
import jax.numpy as jnp
from jax import lax
from jax.experimental import pallas as pl
from jax.experimental.pallas import tpu as pltpu
from jax.sharding import PartitionSpec as P

TILE = 128
TB = 8
KT = 4
OCC = 12
HEAD = 16
PACK = OCC * TILE + HEAD
CUT = OCC // 2 * TILE
EMPTY = 64.0
SIDE = TB * TILE
DEPTH = KT * TILE
BLOCK = 256
VMEM_LIMIT = 20 * 1024 * 1024
PACK_VMEM = 60 * 1024 * 1024
VMEM = pl.BlockSpec(memory_space=pltpu.VMEM)
SMEM = pl.BlockSpec(memory_space=pltpu.SMEM)
HBM = pl.BlockSpec(memory_space=pltpu.HBM)
COST = pl.CostEstimate(flops=1, bytes_accessed=1, transcendentals=0)

X, Y, Z = 4, 8, 12
RUN = 6
HALF_LOOP = 16
N_COL = 32


def device(x, y, z, core):
    z = z % Z
    return (x * RUN + z % RUN) * N_COL + (z // RUN) * HALF_LOOP + (y % Y) * 2 + core


def per_line(*routes):
    return [
        (device(x, y, z, core), device(x, to_y, z + dz, to_core))
        for x in range(X)
        for z in range(Z)
        for (y, core), (to_y, to_core), dz in routes
    ]


HOME = ((0, 0), (0, 1), (1, 0))
VIA = (((0, 1), (7, 1), (1, 1)), ((6, 1), (5, 1), (2, 1)))
GOAL = ((7, 0), (7, 1), (6, 0))


def way(z):
    return -1 if z % 2 == 1 or z == 8 else 1


def to_planes():
    return [
        (device(x, *at(z, home)), device(x, *at(z + way(z), via)))
        for x in range(X)
        for z in range(Z)
        for home, via in zip(HOME, VIA[z // 2 % 2], strict=True)
    ]


def across():
    return [
        (device(x, *at(z + way(z), via)), device(x, *at(z + 6, goal)))
        for x in range(X)
        for z in range(Z)
        for via, goal in zip(VIA[z // 2 % 2], GOAL, strict=True)
    ]


def at(z, place):
    y, core = place
    return y, z, core


def over(source, target):
    (from_dx, from_z), (to_dx, to_z) = source, target
    return [
        (((x + from_dx) % X * RUN + from_z) * N_COL + c, ((x + to_dx) % X * RUN + to_z) * N_COL + c)
        for x in range(X)
        for c in range(N_COL)
    ]


def down(top):
    return [pair for z in range(top) for pair in over((0, z + 1), (0, z))]


def right_hop(distance, within):
    return [
        (q * N_COL + half * HALF_LOOP + c + distance, q * N_COL + half * HALF_LOOP + c)
        for q in range(X * RUN)
        for half in range(2)
        for c in range(within - distance)
    ]


def send(block, route):
    return lax.ppermute(block, ("row", "col"), route)


def after(block, *others):
    return lax.optimization_barrier((block, *others))[0]


def number_slots(mask_at, tile_rows, tile_cols, slots):
    for j in range(OCC):
        slots[j] = 0
    count = jnp.int32(0)
    for i in range(tile_rows):
        for k in range(tile_cols):
            occupied = mask_at(i, k) != 0

            @pl.when(occupied & (count < OCC))
            def _():
                slots[count] = i * tile_cols + k

            count = count + occupied.astype(jnp.int32)
    return jnp.minimum(count, OCC)


def tile_at(tile, tile_cols):
    i = pl.multiple_of(tile // tile_cols * TILE, TILE)
    k = pl.multiple_of(tile % tile_cols * TILE, TILE)
    return pl.ds(i, TILE), pl.ds(k, TILE)


def gather_tiles(source, slots, count, tile_cols, outs):
    lane = lax.broadcasted_iota(jnp.int32, (HEAD, TILE), 1)
    head = jnp.full((HEAD, TILE), EMPTY, jnp.float32)
    for j in range(OCC):
        tile = slots[j]
        data = source[tile_at(tile, tile_cols)]
        for out, base in outs:
            at = j * TILE - base
            if 0 <= at <= out.shape[0] - TILE:
                out[at : at + TILE, :] = data
        head = jnp.where((lane == j) & (j < count), tile.astype(jnp.float32), head)
    for out, base in outs:
        if base + out.shape[0] == PACK:
            out[out.shape[0] - HEAD :, :] = head.astype(jnp.bfloat16)


def pack_kernel(left_mask_across, right_mask, left, right, *refs):
    left_a, left_b, left_all, right_all, left_here, right_here, slots, sems = refs
    left_copy = pltpu.make_async_copy(left, left_here, sems.at[0])
    right_copy = pltpu.make_async_copy(right, right_here, sems.at[1])
    left_copy.start()
    right_copy.start()
    left_count = number_slots(lambda i, k: left_mask_across[k, i], TB, KT, slots.at[0])
    right_count = number_slots(lambda i, k: right_mask[i, k], KT, TB, slots.at[1])
    left_copy.wait()
    gather_tiles(left_here, slots.at[0], left_count, KT, [(left_a, 0), (left_b, CUT), (left_all, 0)])
    right_copy.wait()
    gather_tiles(right_here, slots.at[1], right_count, TB, [(right_all, 0)])


def pack(left_mask, right_mask, left, right):
    return pl.pallas_call(
        pack_kernel,
        out_shape=tuple(jax.ShapeDtypeStruct((n, TILE), jnp.bfloat16) for n in (CUT, PACK - CUT, PACK, PACK)),
        in_specs=[SMEM, SMEM, HBM, HBM],
        out_specs=(VMEM,) * 4,
        scratch_shapes=[
            pltpu.VMEM((SIDE, DEPTH), jnp.bfloat16),
            pltpu.VMEM((DEPTH, SIDE), jnp.bfloat16),
            pltpu.SMEM((2, OCC), jnp.int32),
            pltpu.SemaphoreType.DMA((2,)),
        ],
        compiler_params=pltpu.CompilerParams(vmem_limit_bytes=PACK_VMEM),
        cost_estimate=COST,
        name="pack",
    )(left_mask.T, right_mask, left, right)


def one_of(value, members):
    found = value < 0
    for member in members:
        found = found | (value == member)
    return found


def places_of(choice, wanted):
    z = lax.axis_index("row") % RUN
    c = lax.axis_index("col") % HALF_LOOP
    here = z < 0
    at_c = {at: tuple(k for k in range(HALF_LOOP) if choice[at, k] in wanted) for at in range(RUN)}
    for members in sorted(set(at_c.values())):
        if members:
            rows = one_of(z, [at for at in range(RUN) if at_c[at] == members])
            here = here | (rows if len(members) == HALF_LOOP else rows & one_of(c, members))
    return here


def pick(choice, pieces, use):
    for n, piece in enumerate(pieces):

        @pl.when(places_of(choice, {n}))
        def _(piece=piece):
            use(piece)


def whole(array):
    return ((array, 0), (array, CUT))


def halves(first, second):
    return ((first, 0), (second, 0))


def choose(of):
    arrays, pieces, choice = [], [], {}

    def number(array):
        known = [n for n, other in enumerate(arrays) if other is array]
        if not known:
            arrays.append(array)
        return known[0] if known else len(arrays) - 1

    for z in range(RUN):
        for c in range(HALF_LOOP):
            piece = of(z, c)
            if piece is None:
                choice[z, c] = None
                continue
            piece = tuple((number(array), base) for array, base in piece)
            if piece not in pieces:
                pieces.append(piece)
            choice[z, c] = pieces.index(piece)
    return arrays, pieces, choice


def rows_of(piece, first, n):
    ref, base = piece[first >= CUT]
    first = first - CUT * (first >= CUT) + base
    return ref[first : first + n, :]


def spread_all(work, heads, numbers, sem):
    for n, (choice, refs, _, _) in enumerate(work):

        def read(packed, n=n):
            heads[n] = rows_of(packed, OCC * TILE, HEAD).astype(jnp.float32).astype(jnp.int32)[:8]

        pick(choice, refs, read)
    copy = pltpu.make_async_copy(heads, numbers, sem)
    copy.start()
    for choice, _, dense, _ in work:

        @pl.when(jnp.logical_not(places_of(choice, {None})))
        def _(dense=dense):
            dense[...] = jnp.zeros_like(dense)

    copy.wait()
    for n, (choice, refs, dense, tile_cols) in enumerate(work):

        def place(packed, n=n, dense=dense, tile_cols=tile_cols):
            for j in range(OCC):
                tile = numbers[n, 0, j]

                @pl.when(tile < TB * KT)
                def _():
                    dense[tile_at(tile, tile_cols)] = rows_of(packed, j * TILE, TILE)

        pick(choice, refs, place)


def head_scratch(n):
    return [
        pltpu.VMEM((n, 8, TILE), jnp.int32),
        pltpu.SMEM((n, 8, TILE), jnp.int32),
        pltpu.SemaphoreType.DMA(()),
    ]


def take(refs, n):
    return [refs.pop(0) for _ in range(n)]


def take_pieces(refs, chosen):
    arrays, pieces, _ = chosen
    here = take(refs, len(arrays))
    return [tuple((here[n], base) for n, base in piece) for piece in pieces]


def multiply(total, steps, last):
    first, n = total is None, len(steps)
    skips = [step[0][2] for step in steps]
    sometimes = [at for at in range(n) if None in skips[at].values()]
    always = n - len(sometimes)
    assert sometimes == list(range(always, n))

    def kernel(*refs):
        refs = list(refs)
        before = None if first else refs.pop(0)
        inputs = [(take_pieces(refs, left), take_pieces(refs, right)) for left, right in steps]
        out, left, right, heads, numbers, sem = take(refs, 6)
        work = []
        for at, (left_in, right_in) in enumerate(inputs):
            inner = pl.ds(at * DEPTH, DEPTH)
            work.append((steps[at][0][2], left_in, left.at[:, inner], KT))
            work.append((steps[at][1][2], right_in, right.at[inner, :], TB))
        spread_all(work, heads, numbers, sem)
        rounded, sems = refs if last else (None, None)

        def add_up(rows, depth, then):
            part = jnp.dot(left[rows, :depth], right[:depth, :], preferred_element_type=jnp.float32)
            then(rows, part if first else before[rows, :] + part)

        def each_block(depth, then):
            for block in range(SIDE // BLOCK):
                add_up(pl.ds(block * BLOCK, BLOCK), depth, then)

        def keep(rows, value):
            out[rows, :] = value

        def write(rows, value):
            at = rows.start // BLOCK
            rounded[rows, :] = value.astype(jnp.bfloat16)
            pltpu.make_async_copy(rounded.at[rows, :], out.at[rows, :], sems.at[at]).start()

        then = write if last else keep
        if sometimes:
            skipped = places_of(skips[always], {None})

            @pl.when(skipped)
            def _():
                each_block(always * DEPTH, then)

            @pl.when(jnp.logical_not(skipped))
            def _():
                each_block(n * DEPTH, then)

        else:
            each_block(n * DEPTH, then)
        if last:
            for block in range(SIDE // BLOCK):
                rows = pl.ds(block * BLOCK, BLOCK)
                pltpu.make_async_copy(rounded.at[rows, :], out.at[rows, :], sems.at[block]).wait()

    args = [] if first else [total]
    for left, right in steps:
        args += left[0] + right[0]
    scratch = [
        pltpu.VMEM((SIDE, n * DEPTH), jnp.bfloat16),
        pltpu.VMEM((n * DEPTH, SIDE), jnp.bfloat16),
    ] + head_scratch(2 * n)
    if last:
        scratch += [
            pltpu.VMEM((SIDE, SIDE), jnp.bfloat16),
            pltpu.SemaphoreType.DMA((SIDE // BLOCK,)),
        ]
    return pl.pallas_call(
        kernel,
        out_shape=jax.ShapeDtypeStruct((SIDE, SIDE), jnp.bfloat16 if last else jnp.float32),
        in_specs=[VMEM] * len(args),
        out_specs=HBM if last else VMEM,
        scratch_shapes=scratch,
        compiler_params=pltpu.CompilerParams(vmem_limit_bytes=VMEM_LIMIT),
        cost_estimate=COST,
        name="finish" if last else "multiply",
    )(*args)


def local(left_factor, left_mask, right_factor, right_mask):
    la, lb, l0, r0 = pack(left_mask, right_mask, left_factor, right_factor)

    ring = down(5) + over((1, 0), (0, 5))
    first_a, first_b = send(la, ring), send(lb, ring)
    over_both = send(l0, over((1, 1), (0, 5)) + over((1, 2), (0, 4)))
    second_a, second_b = send(first_a, down(5)), send(first_b, down(5))
    moved = send(r0, to_planes())
    crossed = send(moved, across())
    n1 = send(r0, right_hop(1, 16))
    n2 = send(r0, right_hop(2, 16))
    n3 = send(n2, right_hop(1, 14))

    def early(c):
        return c < 15

    lefts = {
        1: [halves(first_a, first_b)] * 6,
        2: [halves(second_a, second_b)] * 5 + [whole(over_both)],
    }
    third = send(after(jnp.concatenate([second_a, second_b]), over_both), down(4))
    changed = send(over_both, over((0, 5), (0, 4)) + over((0, 4), (0, 5)))
    lefts[3] = [whole(third)] * 4 + [whole(changed)] * 2
    crossed_late = after(crossed, over_both)
    g1 = send(crossed_late, per_line(((7, 0), (7, 1), 0)))
    g2 = send(crossed_late, per_line(((7, 0), (6, 1), 0), ((7, 1), (7, 0), 0), ((6, 0), (7, 1), 0)))

    def right_of(step, c):
        return whole({1: (n1, g1), 2: (n2, crossed), 3: (n3, g2)}[step][c + step >= HALF_LOOP])

    def step_of(step, when=None):
        return (
            choose(lambda z, c: lefts[step][z] if when is None or when(c) else None),
            choose(lambda z, c: right_of(step, c) if when is None or when(c) else None),
        )

    own = (choose(lambda z, c: whole(l0)), choose(lambda z, c: whole(r0)))
    total = multiply(None, [own, step_of(2), step_of(1, early)], False)
    return multiply(total, [step_of(3), step_of(1, lambda c: not early(c))], True)


def solution(mesh):
    placed = (P("col", "row"), P("col", "row"), P("col", "row"), P("col", "row"))
    return jax.shard_map(
        local, mesh=mesh, in_specs=placed, out_specs=P("col", "row"), check_vma=False
    )
```

```python
import jax
import jax.numpy as jnp
from jax import lax
from jax.experimental import pallas as pl
from jax.experimental.pallas import tpu as pltpu
from jax.sharding import PartitionSpec as P

TILE = 128
TB = 8
KT = 4
OCC = 12
HEAD = 16
PACK = OCC * TILE + HEAD
CUT = OCC // 2 * TILE
EMPTY = 64.0
SIDE = TB * TILE
DEPTH = KT * TILE
BLOCK = 256
VMEM_LIMIT = 20 * 1024 * 1024
PACK_VMEM = 60 * 1024 * 1024
VMEM = pl.BlockSpec(memory_space=pltpu.VMEM)
SMEM = pl.BlockSpec(memory_space=pltpu.SMEM)
HBM = pl.BlockSpec(memory_space=pltpu.HBM)
COST = pl.CostEstimate(flops=1, bytes_accessed=1, transcendentals=0)

X, Y, Z = 4, 8, 12
RUN = 6
HALF_LOOP = 16
N_COL = 32


def device(x, y, z, core):
    z = z % Z
    return (x * RUN + z % RUN) * N_COL + (z // RUN) * HALF_LOOP + (y % Y) * 2 + core


def per_line(*routes):
    return [
        (device(x, y, z, core), device(x, to_y, z + dz, to_core))
        for x in range(X)
        for z in range(Z)
        for (y, core), (to_y, to_core), dz in routes
    ]


HOME = ((0, 0), (0, 1), (1, 0))
VIA = (((0, 1), (7, 1), (1, 1)), ((6, 1), (5, 1), (2, 1)), ((3, 1), (4, 1), (3, 0)))
GOAL = ((7, 0), (7, 1), (6, 0))


def way(z):
    return -1 if z % 2 == 1 or z == 8 else 1


def planes(z):
    return 2 if z in (8, 9) else z // 2 % 2


def to_planes():
    return [
        (device(x, *at(z, home)), device(x, *at(z + way(z), via)))
        for x in range(X)
        for z in range(Z)
        for home, via in zip(HOME, VIA[planes(z)], strict=True)
    ]


def across():
    return [
        (device(x, *at(z + way(z), via)), device(x, *at(z + 6, goal)))
        for x in range(X)
        for z in range(Z)
        for via, goal in zip(VIA[planes(z)], GOAL, strict=True)
    ]


def at(z, place):
    y, core = place
    return y, z, core


def over(source, target):
    (from_dx, from_z), (to_dx, to_z) = source, target
    return [
        (((x + from_dx) % X * RUN + from_z) * N_COL + c, ((x + to_dx) % X * RUN + to_z) * N_COL + c)
        for x in range(X)
        for c in range(N_COL)
    ]


def down(top):
    return [pair for z in range(top) for pair in over((0, z + 1), (0, z))]


def right_hop(distance, within):
    return [
        (q * N_COL + half * HALF_LOOP + c + distance, q * N_COL + half * HALF_LOOP + c)
        for q in range(X * RUN)
        for half in range(2)
        for c in range(within - distance)
    ]


def send(block, route):
    return lax.ppermute(block, ("row", "col"), route)


def after(block, *others):
    return lax.optimization_barrier((block, *others))[0]


def number_slots(mask_at, tile_rows, tile_cols, slots):
    for j in range(OCC):
        slots[j] = 0
    count = jnp.int32(0)
    for i in range(tile_rows):
        for k in range(tile_cols):
            occupied = mask_at(i, k) != 0

            @pl.when(occupied & (count < OCC))
            def _():
                slots[count] = i * tile_cols + k

            count = count + occupied.astype(jnp.int32)
    return jnp.minimum(count, OCC)


def tile_at(tile, tile_cols):
    i = pl.multiple_of(tile // tile_cols * TILE, TILE)
    k = pl.multiple_of(tile % tile_cols * TILE, TILE)
    return pl.ds(i, TILE), pl.ds(k, TILE)


def gather_tiles(source, slots, count, tile_cols, outs):
    lane = lax.broadcasted_iota(jnp.int32, (HEAD, TILE), 1)
    head = jnp.full((HEAD, TILE), EMPTY, jnp.float32)
    for j in range(OCC):
        tile = slots[j]
        data = source[tile_at(tile, tile_cols)]
        for out, base in outs:
            at = j * TILE - base
            if 0 <= at <= out.shape[0] - TILE:
                out[at : at + TILE, :] = data
        head = jnp.where((lane == j) & (j < count), tile.astype(jnp.float32), head)
    for out, base in outs:
        if base + out.shape[0] == PACK:
            out[out.shape[0] - HEAD :, :] = head.astype(jnp.bfloat16)


def pack_kernel(left_mask_across, right_mask, left, right, *refs):
    left_a, left_b, left_all, right_all, left_here, right_here, slots, sems = refs
    left_copy = pltpu.make_async_copy(left, left_here, sems.at[0])
    right_copy = pltpu.make_async_copy(right, right_here, sems.at[1])
    left_copy.start()
    right_copy.start()
    left_count = number_slots(lambda i, k: left_mask_across[k, i], TB, KT, slots.at[0])
    right_count = number_slots(lambda i, k: right_mask[i, k], KT, TB, slots.at[1])
    left_copy.wait()
    gather_tiles(left_here, slots.at[0], left_count, KT, [(left_a, 0), (left_b, CUT), (left_all, 0)])
    right_copy.wait()
    gather_tiles(right_here, slots.at[1], right_count, TB, [(right_all, 0)])


def pack(left_mask, right_mask, left, right):
    return pl.pallas_call(
        pack_kernel,
        out_shape=tuple(jax.ShapeDtypeStruct((n, TILE), jnp.bfloat16) for n in (CUT, PACK - CUT, PACK, PACK)),
        in_specs=[SMEM, SMEM, HBM, HBM],
        out_specs=(VMEM,) * 4,
        scratch_shapes=[
            pltpu.VMEM((SIDE, DEPTH), jnp.bfloat16),
            pltpu.VMEM((DEPTH, SIDE), jnp.bfloat16),
            pltpu.SMEM((2, OCC), jnp.int32),
            pltpu.SemaphoreType.DMA((2,)),
        ],
        compiler_params=pltpu.CompilerParams(vmem_limit_bytes=PACK_VMEM),
        cost_estimate=COST,
        name="pack",
    )(left_mask.T, right_mask, left, right)


def one_of(value, members):
    found = value < 0
    for member in members:
        found = found | (value == member)
    return found


def places_of(choice, wanted):
    z = lax.axis_index("row") % RUN
    c = lax.axis_index("col") % HALF_LOOP
    here = z < 0
    at_c = {at: tuple(k for k in range(HALF_LOOP) if choice[at, k] in wanted) for at in range(RUN)}
    for members in sorted(set(at_c.values())):
        if members:
            rows = one_of(z, [at for at in range(RUN) if at_c[at] == members])
            here = here | (rows if len(members) == HALF_LOOP else rows & one_of(c, members))
    return here


def pick(choice, pieces, use):
    for n, piece in enumerate(pieces):

        @pl.when(places_of(choice, {n}))
        def _(piece=piece):
            use(piece)


def whole(array):
    return ((array, 0), (array, CUT))


def halves(first, second):
    return ((first, 0), (second, 0))


def choose(of):
    arrays, pieces, choice = [], [], {}

    def number(array):
        known = [n for n, other in enumerate(arrays) if other is array]
        if not known:
            arrays.append(array)
        return known[0] if known else len(arrays) - 1

    for z in range(RUN):
        for c in range(HALF_LOOP):
            piece = of(z, c)
            if piece is None:
                choice[z, c] = None
                continue
            piece = tuple((number(array), base) for array, base in piece)
            if piece not in pieces:
                pieces.append(piece)
            choice[z, c] = pieces.index(piece)
    return arrays, pieces, choice


def rows_of(piece, first, n):
    ref, base = piece[first >= CUT]
    first = first - CUT * (first >= CUT) + base
    return ref[first : first + n, :]


def spread_all(work, heads, numbers, sem):
    for n, (choice, refs, _, _) in enumerate(work):

        def read(packed, n=n):
            heads[n] = rows_of(packed, OCC * TILE, HEAD).astype(jnp.float32).astype(jnp.int32)[:8]

        pick(choice, refs, read)
    copy = pltpu.make_async_copy(heads, numbers, sem)
    copy.start()
    for choice, _, dense, _ in work:

        @pl.when(jnp.logical_not(places_of(choice, {None})))
        def _(dense=dense):
            dense[...] = jnp.zeros_like(dense)

    copy.wait()
    for n, (choice, refs, dense, tile_cols) in enumerate(work):

        def place(packed, n=n, dense=dense, tile_cols=tile_cols):
            for j in range(OCC):
                tile = numbers[n, 0, j]

                @pl.when(tile < TB * KT)
                def _():
                    dense[tile_at(tile, tile_cols)] = rows_of(packed, j * TILE, TILE)

        pick(choice, refs, place)


def head_scratch(n):
    return [
        pltpu.VMEM((n, 8, TILE), jnp.int32),
        pltpu.SMEM((n, 8, TILE), jnp.int32),
        pltpu.SemaphoreType.DMA(()),
    ]


def take(refs, n):
    return [refs.pop(0) for _ in range(n)]


def take_pieces(refs, chosen):
    arrays, pieces, _ = chosen
    here = take(refs, len(arrays))
    return [tuple((here[n], base) for n, base in piece) for piece in pieces]


def multiply(total, steps, last):
    first, n = total is None, len(steps)
    skips = [step[0][2] for step in steps]
    sometimes = [at for at in range(n) if None in skips[at].values()]
    always = n - len(sometimes)
    assert sometimes == list(range(always, n))

    def kernel(*refs):
        refs = list(refs)
        before = None if first else refs.pop(0)
        inputs = [(take_pieces(refs, left), take_pieces(refs, right)) for left, right in steps]
        out, left, right, heads, numbers, sem = take(refs, 6)
        work = []
        for at, (left_in, right_in) in enumerate(inputs):
            inner = pl.ds(at * DEPTH, DEPTH)
            work.append((steps[at][0][2], left_in, left.at[:, inner], KT))
            work.append((steps[at][1][2], right_in, right.at[inner, :], TB))
        spread_all(work, heads, numbers, sem)
        rounded, sems = refs if last else (None, None)

        def add_up(rows, depth, then):
            part = jnp.dot(left[rows, :depth], right[:depth, :], preferred_element_type=jnp.float32)
            then(rows, part if first else before[rows, :] + part)

        def each_block(depth, then):
            for block in range(SIDE // BLOCK):
                add_up(pl.ds(block * BLOCK, BLOCK), depth, then)

        def keep(rows, value):
            out[rows, :] = value

        def write(rows, value):
            at = rows.start // BLOCK
            rounded[rows, :] = value.astype(jnp.bfloat16)
            pltpu.make_async_copy(rounded.at[rows, :], out.at[rows, :], sems.at[at]).start()

        then = write if last else keep
        if sometimes:
            skipped = places_of(skips[always], {None})

            @pl.when(skipped)
            def _():
                each_block(always * DEPTH, then)

            @pl.when(jnp.logical_not(skipped))
            def _():
                each_block(n * DEPTH, then)

        else:
            each_block(n * DEPTH, then)
        if last:
            for block in range(SIDE // BLOCK):
                rows = pl.ds(block * BLOCK, BLOCK)
                pltpu.make_async_copy(rounded.at[rows, :], out.at[rows, :], sems.at[block]).wait()

    args = [] if first else [total]
    for left, right in steps:
        args += left[0] + right[0]
    scratch = [
        pltpu.VMEM((SIDE, n * DEPTH), jnp.bfloat16),
        pltpu.VMEM((n * DEPTH, SIDE), jnp.bfloat16),
    ] + head_scratch(2 * n)
    if last:
        scratch += [
            pltpu.VMEM((SIDE, SIDE), jnp.bfloat16),
            pltpu.SemaphoreType.DMA((SIDE // BLOCK,)),
        ]
    return pl.pallas_call(
        kernel,
        out_shape=jax.ShapeDtypeStruct((SIDE, SIDE), jnp.bfloat16 if last else jnp.float32),
        in_specs=[VMEM] * len(args),
        out_specs=HBM if last else VMEM,
        scratch_shapes=scratch,
        compiler_params=pltpu.CompilerParams(vmem_limit_bytes=VMEM_LIMIT),
        cost_estimate=COST,
        name="finish" if last else "multiply",
    )(*args)


def local(left_factor, left_mask, right_factor, right_mask):
    la, lb, l0, r0 = pack(left_mask, right_mask, left_factor, right_factor)

    ring = down(5) + over((1, 0), (0, 5))
    first_a, first_b = send(la, ring), send(lb, ring)
    over_both = send(l0, over((1, 1), (0, 5)) + over((1, 2), (0, 4)))
    second_a, second_b = send(first_a, down(5)), send(first_b, down(5))
    moved = send(r0, to_planes())
    crossed = send(moved, across())
    n1 = send(r0, right_hop(1, 16))
    n2 = send(r0, right_hop(2, 16))
    n3 = send(n2, right_hop(1, 14))

    def early(c):
        return c < 15

    lefts = {
        1: [halves(first_a, first_b)] * 6,
        2: [halves(second_a, second_b)] * 5 + [whole(over_both)],
    }
    third = send(after(jnp.concatenate([second_a, second_b]), over_both), down(4))
    changed = send(over_both, over((0, 5), (0, 4)) + over((0, 4), (0, 5)))
    lefts[3] = [whole(third)] * 4 + [whole(changed)] * 2
    crossed_late = after(crossed, over_both)
    g1 = send(crossed_late, per_line(((7, 0), (7, 1), 0)))
    g2 = send(crossed_late, per_line(((7, 0), (6, 1), 0), ((7, 1), (7, 0), 0), ((6, 0), (7, 1), 0)))

    def right_of(step, c):
        return whole({1: (n1, g1), 2: (n2, crossed), 3: (n3, g2)}[step][c + step >= HALF_LOOP])

    def step_of(step, when=None):
        return (
            choose(lambda z, c: lefts[step][z] if when is None or when(c) else None),
            choose(lambda z, c: right_of(step, c) if when is None or when(c) else None),
        )

    own = (choose(lambda z, c: whole(l0)), choose(lambda z, c: whole(r0)))
    total = multiply(None, [own, step_of(2), step_of(1, early)], False)
    return multiply(total, [step_of(3), step_of(1, lambda c: not early(c))], True)


def solution(mesh):
    placed = (P("col", "row"), P("col", "row"), P("col", "row"), P("col", "row"))
    return jax.shard_map(
        local, mesh=mesh, in_specs=placed, out_specs=P("col", "row"), check_vma=False
    )
```
